32 devices in a mesh: grp: 4 (over y, x), mem: 8 (over z, core).
Axes of the slice: x: 2, y: 2, z: 4, core: 2. Of those that a mesh axis runs over, the one named last changes fastest.
Arguments:
- features: bfloat16 [131072, 1024], P(('grp', 'mem')), may hold values from -24 to 24
- lengths: int32 [32, 2], P(('grp', 'mem')), may hold values from 512 to 2048, as said below
Outputs:
- sample_count: float32 [1], replicated
- feature_mean: float32 [1024], replicated
- covariance: float32 [1024, 1024], P(('grp', 'mem'))
The draws below stay inside these ranges and needn't reach their ends.
Inputs may be any that keep to these rules, and one draw needn't show every extreme that they name: Every block of a device has 2048 slots; lengths count the valid leading slots.
All inputs are finite; a program needn't handle non-finite values.
Results may differ from the reference program's by a relative error of at most 0.0003.
Values sent between devices are 32-bit elements; how exact they have to be, the bound alone decides.
No kernel may reach another device: no remote copies, remote signals or barrier semaphores. Data moves between devices by JAX's collectives and lax.ppermute only.
A program may use at most 64 MiB of HBM per device.

```python
import jax
import jax.numpy as jnp
from jax import lax

D = 1024
BLOCK_ROWS = 2048
SHARDS = 32
IMAGES = 131072


def draw_features(key, part):
    key_scale = jax.random.fold_in(key, 11)
    key_offset = jax.random.fold_in(key, 12)
    key_noise = jax.random.fold_in(key, 13)
    scales = 0.3 * jnp.exp(jax.random.uniform(key_scale, (D,), jnp.float32, 0.0, jnp.log(10.0)))
    offsets = jnp.clip(jax.random.normal(key_offset, (D,), jnp.float32), -3.0, 3.0)
    noise = jnp.clip(jax.random.normal(key_noise, (IMAGES, D), jnp.float32), -6.0, 6.0)
    return (noise * scales[None, :] + offsets[None, :]).astype(jnp.bfloat16)


def draw_lengths(key, part):
    index = jnp.arange(SHARDS, dtype=jnp.int32)
    upper = BLOCK_ROWS // 4 + 1 + 3 * BLOCK_ROWS // 4 * (index + 1) // SHARDS
    values = jax.random.randint(key, (SHARDS, 2), BLOCK_ROWS // 4, upper[:, None])
    values = values.at[0, 0].set(BLOCK_ROWS // 4)
    values = values.at[SHARDS - 1, 1].set(BLOCK_ROWS)
    return values.astype(jnp.int32)


def setup_inputs(seed: int = 0) -> dict:
    seeds = jax.random.split(jax.random.key(seed), 3)
    features = draw_features(jax.random.fold_in(seeds[2], 71), 0)
    lengths = draw_lengths(jax.random.fold_in(seeds[2], 71), 0)
    return {"features": features, "lengths": lengths}


def reference(features, lengths):
    total = jnp.sum(lengths).astype(jnp.float32)
    blocks = features.reshape(SHARDS * 2, BLOCK_ROWS, D)
    position = jnp.arange(BLOCK_ROWS, dtype=jnp.int32)
    weights = (position[None, :] < lengths.reshape(SHARDS * 2, 1)).astype(jnp.float32)

    def add_sum(acc, item):
        block, mask = item
        return acc + jnp.sum(block.astype(jnp.float32) * mask[:, None], axis=0), None

    sums, _ = lax.scan(add_sum, jnp.zeros((D,), jnp.float32), (blocks, weights))
    feature_mean = sums / total

    def add_gram(acc, item):
        block, mask = item
        centred = (block.astype(jnp.float32) - feature_mean[None, :]) * mask[:, None]
        return acc + jnp.dot(centred.T, centred, precision=lax.Precision.HIGHEST), None

    second, _ = lax.scan(add_gram, jnp.zeros((D, D), jnp.float32), (blocks, weights))
    covariance = second / (total - 1.0)
    return total.reshape(1), feature_mean, covariance
```

```python
import functools

import jax
import jax.numpy as jnp
from jax import lax
from jax.experimental import pallas as pl
from jax.experimental.pallas import tpu as pltpu
from jax.sharding import PartitionSpec as P

LANES = 128
SUBLANES = 8


def exchange_masks(groups, members):
    core, others = 1, []
    for bit in range(groups.bit_length() - 1):
        others.append(members << bit)
    for bit in range(1, members.bit_length() - 1):
        others.append(1 << bit if bit % 2 else 3 << (bit - 1))
    return core, others


def exchange_orders(others, width):
    portions = 1
    while 2 * portions <= len(others) and width % (2 * portions * LANES) == 0:
        portions *= 2
    step = max(1, len(others) // portions)
    return [others[i * step:] + others[:i * step] for i in range(portions)]


def relative(order, place):
    device = 0
    for i, mask in enumerate(order):
        if not place >> (len(order) - 1 - i) & 1:
            device ^= mask
    return device


def gram_kernel(me_ref, len_ref, x_hbm, mine_ref, theirs_ref, extra_ref,
                x_ref, acc_ref, sem, *, tile, core, orders, rows):
    depth, width = x_hbm.shape
    half_tiles = depth // 2 // tile

    def fetch(i):
        part = pl.ds(i * tile, tile)
        return pltpu.make_async_copy(x_hbm.at[part], x_ref.at[part], sem.at[i])

    for i in range(2 * half_tiles):
        fetch(i).start()
    total = jnp.zeros((1, width), jnp.float32)
    for i in range(2 * half_tiles):
        fetch(i).wait()
        valid = len_ref[i // half_tiles] - (i % half_tiles) * tile
        x = x_ref[pl.ds(i * tile, tile), :]
        position = lax.broadcasted_iota(jnp.int32, x.shape, 0)
        masked = jnp.where(position < valid, x, jnp.zeros_like(x))
        total += jnp.sum(masked.astype(jnp.float32), axis=0, keepdims=True)
        product = lax.dot_general(
            masked, x, (((0,), (0,)), ((), ())), preferred_element_type=jnp.float32
        )
        if i:
            acc_ref[...] += product
        else:
            acc_ref[...] = product
    me = me_ref[0]
    columns = width // len(orders)
    for p, order in enumerate(orders):
        places = 1 << len(order)
        for place in range(places):
            device = relative(order, place)
            out = pl.ds((p * places + place) * rows, rows)
            for ref, mask in ((mine_ref, device), (theirs_ref, device ^ core)):
                source = pl.ds(pl.multiple_of((me ^ mask) * rows, rows), rows)
                ref[out, :] = acc_ref[source, pl.ds(p * columns, columns)]
    count = (len_ref[0] + len_ref[1]).astype(jnp.float32)
    for i in range(width // LANES):
        extra_ref[pl.ds(i, 1), :] = total[:, i * LANES:(i + 1) * LANES]
    extra_ref[pl.ds(width // LANES, SUBLANES), :] = jnp.full((SUBLANES, LANES), count)


def gram(me, lengths, x, core, orders, rows, tile=1024):
    depth, width = x.shape
    columns = width // len(orders)
    half = jax.ShapeDtypeStruct((width // 2 * len(orders), columns), jnp.float32)
    extra = jax.ShapeDtypeStruct((width // LANES + SUBLANES, LANES), jnp.float32)
    smem = pl.BlockSpec(memory_space=pltpu.SMEM)
    vmem = pl.BlockSpec(memory_space=pltpu.VMEM)
    return pl.pallas_call(
        functools.partial(gram_kernel, tile=tile, core=core, orders=orders, rows=rows),
        out_shape=[half, half, extra],
        in_specs=[smem, smem, pl.BlockSpec(memory_space=pl.ANY)],
        out_specs=[vmem, vmem, vmem],
        scratch_shapes=[
            pltpu.VMEM((depth, width), x.dtype),
            pltpu.VMEM((width, width), jnp.float32),
            pltpu.SemaphoreType.DMA((depth // tile,)),
        ],
        compiler_params=pltpu.CompilerParams(vmem_limit_bytes=40 << 20),
        cost_estimate=pl.CostEstimate(
            flops=2 * depth * width * width, bytes_accessed=depth * width * 2, transcendentals=0
        ),
    )(me, lengths, x)


def finish_kernel(me_ref, extra_ref, *refs, rows, terms):
    portions = len(refs) // terms
    pieces, (cov_ref, mean_ref, count_ref) = refs[:-3], refs[-3:]
    width = cov_ref.shape[1]
    tiles = width // LANES
    count = extra_ref[tiles:tiles + 1, 0:1]
    total = jnp.concatenate([extra_ref[i:i + 1, :] for i in range(tiles)], axis=1)
    lane = lax.broadcasted_iota(jnp.int32, (rows, width), 1)
    row = lax.broadcasted_iota(jnp.int32, (rows, width), 0)
    own = jnp.sum(
        jnp.where(lane == row + me_ref[0] * rows, total, 0.0), axis=1, keepdims=True
    )
    mean = total / count
    mean_ref[...] = mean
    count_ref[...] = count
    columns = width // portions
    for p in range(portions):
        part = pieces[p * terms][...]
        for ref in pieces[p * terms + 1:(p + 1) * terms]:
            part += ref[...]
        at = slice(p * columns, (p + 1) * columns)
        cov_ref[:, at] = (part - own * mean[:, at]) / (count - 1.0)


def finish(me, extra, pieces, rows, width):
    terms = len(pieces[0])
    return pl.pallas_call(
        functools.partial(finish_kernel, rows=rows, terms=terms),
        out_shape=[
            jax.ShapeDtypeStruct((rows, width), jnp.float32),
            jax.ShapeDtypeStruct((1, width), jnp.float32),
            jax.ShapeDtypeStruct((1, 1), jnp.float32),
        ],
        in_specs=[pl.BlockSpec(memory_space=pltpu.SMEM)]
        + [pl.BlockSpec(memory_space=pltpu.VMEM)] * (1 + terms * len(pieces)),
        out_specs=[pl.BlockSpec(memory_space=pltpu.VMEM)] * 3,
    )(me, extra, *[term for piece in pieces for term in piece])


def solution(mesh):
    axes = ("grp", "mem")
    groups, members = mesh.shape["grp"], mesh.shape["mem"]
    devices = groups * members
    core, others = exchange_masks(groups, members)

    def swap(value, mask):
        return lax.ppermute(value, axes, [(i, i ^ mask) for i in range(devices)])

    def body(features, lengths):
        width = features.shape[1]
        rows = width // devices
        orders = exchange_orders(others, width)
        places = 1 << len(others)
        me = (lax.axis_index("grp") * members + lax.axis_index("mem")).reshape(1)
        mine, theirs, extra = gram(me, lengths[0], features, core, orders, rows)
        other = swap(theirs, core)
        for mask in [core] + others:
            extra = extra + swap(extra, mask)
        parts = []
        for p in range(len(orders)):
            at = slice(p * places * rows, (p + 1) * places * rows)
            parts.append([mine[at], other[at]])
        for step in range(len(others)):
            send = places >> (step + 1)
            for p, order in enumerate(orders):
                message = sum(part[:send * rows] for part in parts[p])
                arrived = swap(message, order[step])
                parts[p] = [part[send * rows:] for part in parts[p]] + [arrived]
        covariance, mean, count = finish(me, extra, parts, rows, width)
        return count.reshape(1), mean.reshape(width), covariance

    return jax.shard_map(
        body,
        mesh=mesh,
        in_specs=(P(axes, None), P(axes, None)),
        out_specs=(P(), P(), P(axes, None)),
        check_vma=False,
    )
```

```python
import functools

import jax
import jax.numpy as jnp
from jax import lax
from jax.experimental import pallas as pl
from jax.experimental.pallas import tpu as pltpu
from jax.sharding import PartitionSpec as P

LANES = 128
EXTRA = 8
CORE = 1
SMEM = pl.BlockSpec(memory_space=pltpu.SMEM)
VMEM = pl.BlockSpec(memory_space=pltpu.VMEM)
ANY = pl.BlockSpec(memory_space=pl.ANY)


def exchange_masks(groups, members):
    masks = [members << bit for bit in range(groups.bit_length() - 1)]
    return masks + [1 << bit for bit in range(1, members.bit_length() - 1)]


def column_portions(masks, width):
    heads, tail = masks[:3], masks[3:]
    tiles = width // LANES
    portions, start = [], 0
    for i in range(len(heads)):
        size = (tiles + len(heads) - 1 - i) // len(heads) * LANES
        portions.append((start, size, heads[i:] + heads[:i] + tail))
        start += size
    return portions


def mirror(acc_ref, done, count, block):
    for n in range(count):
        for other in range(n):
            at = slice(n * block, (n + 1) * block)
            left = slice((done + other) * block, (done + other + 1) * block)
            above = slice(other * block, (other + 1) * block)
            right = slice((done + n) * block, (done + n + 1) * block)
            acc_ref[at, left] = acc_ref[above, right].T


def gram_rows(order, done, count, acc_ref, me, outs, groups, members, rows):
    group, member = me // members, me % members
    block = members * rows
    place = 0
    for n in range(count):
        for j in range(0, members, 2):
            for out, mask in zip(outs, (j, j ^ CORE)):
                source = pl.ds(pl.multiple_of(n * block + (member ^ mask) * rows, rows), rows)
                for other, key in enumerate(order):
                    columns = pl.ds(pl.multiple_of((group ^ key) * block, block), block)
                    out[pl.ds(place * rows, rows), columns] = (
                        acc_ref[source, other * block:(other + 1) * block]
                    )
            place += 1


def transposed_dot(a, b):
    return lax.dot_general(a, b, (((0,), (0,)), ((), ())), preferred_element_type=jnp.float32)


def first_kernel(me_ref, len_ref, x_hbm, mine_ref, theirs_ref, x_ref, acc_ref, sums_ref, sem,
                 *, tile, order, count, groups, members, rows, pack):
    depth, width = x_hbm.shape
    block = width // groups
    half_tiles = depth // 2 // tile
    me = me_ref[0]
    group = me // members

    for i in range(2 * half_tiles):
        part = pl.ds(i * tile, tile)
        for n, key in enumerate(order):
            columns = pl.ds(pl.multiple_of((group ^ key) * block, block), block)
            pltpu.make_async_copy(
                x_hbm.at[part, columns], x_ref.at[part, pl.ds(n * block, block)], sem.at[i]
            ).start()
    total = jnp.zeros((1, width), jnp.float32)
    for i in range(2 * half_tiles):
        part = pl.ds(i * tile, tile)
        pltpu.make_async_copy(x_hbm.at[part], x_ref.at[part], sem.at[i]).wait()
        valid = len_ref[i // half_tiles] - (i % half_tiles) * tile

        @pl.when(valid < tile)
        def _():
            x = x_ref[part, :]
            position = lax.broadcasted_iota(jnp.int32, x.shape, 0)
            x_ref[part, :] = jnp.where(position < valid, x, jnp.zeros_like(x))

        total += jnp.sum(x_ref[part, :].astype(jnp.float32), axis=0, keepdims=True)
        for n in range(count):
            product = transposed_dot(x_ref[part, n * block:(n + 1) * block], x_ref[part, n * block:])
            at = pl.ds(n * block, block), pl.ds(n * block, width - n * block)
            if i:
                acc_ref[at] += product
            else:
                acc_ref[at] = product
    mirror(acc_ref, 0, count, block)
    gram_rows(order, 0, count, acc_ref, me, (mine_ref, theirs_ref), groups, members, rows)
    images = (len_ref[0] + len_ref[1]).astype(jnp.float32)
    for n, key in enumerate(order):
        columns = pl.ds(pl.multiple_of((group ^ key) * block, block), block)
        sums_ref[0:1, columns] = total[:, n * block:(n + 1) * block]
    at = count * members // 2 * rows
    for ref in (mine_ref, theirs_ref):
        ref[pl.ds(at, EXTRA), :] = jnp.full((EXTRA, width), images)
        for line, start in enumerate(range(0, width, pack)):
            size = min(pack, width - start)
            ref[pl.ds(at + line, 1), pl.ds(0, size)] = sums_ref[0:1, start:start + size]


def second_kernel(me_ref, x_ref, done_ref, mine_ref, theirs_ref, acc_ref,
                  *, order, count, groups, members, rows):
    width = x_ref.shape[1]
    block = width // groups
    done = done_ref.shape[0] // block
    for n in range(done, done + count):
        at = slice((n - done) * block, (n - done + 1) * block)
        for other in range(done):
            acc_ref[at, other * block:(other + 1) * block] = (
                done_ref[other * block:(other + 1) * block, n * block:(n + 1) * block].T
            )
        acc_ref[at, n * block:] = transposed_dot(
            x_ref[:, n * block:(n + 1) * block], x_ref[:, n * block:]
        )
    mirror(acc_ref, done, count, block)
    gram_rows(order, done, count, acc_ref, me_ref[0], (mine_ref, theirs_ref), groups, members, rows)


def grams(me, lengths, x, groups, members, pack, tile=1024):
    depth, width = x.shape
    block, rows = width // groups, width // groups // members
    first = [key for key in reversed(range(groups)) if key & 1]
    second = [key for key in reversed(range(groups)) if not key & 1]

    def half(keys, extra):
        return jax.ShapeDtypeStruct((len(keys) * block // 2 + extra, width), jnp.float32)

    def cost(blocks):
        return pl.CostEstimate(
            flops=2 * depth * block * block * blocks,
            bytes_accessed=depth * width * 2,
            transcendentals=0,
        )

    sizes = dict(order=first + second, groups=groups, members=members, rows=rows)
    mine, theirs, kept, done = pl.pallas_call(
        functools.partial(first_kernel, tile=tile, count=len(first), pack=pack, **sizes),
        out_shape=[half(first, EXTRA)] * 2
        + [
            jax.ShapeDtypeStruct(x.shape, x.dtype),
            jax.ShapeDtypeStruct((len(first) * block, width), jnp.float32),
        ],
        in_specs=[SMEM, SMEM, ANY],
        out_specs=[VMEM] * 4,
        scratch_shapes=[
            pltpu.VMEM((EXTRA, width), jnp.float32),
            pltpu.SemaphoreType.DMA((depth // tile,)),
        ],
        compiler_params=pltpu.CompilerParams(vmem_limit_bytes=40 << 20),
        cost_estimate=cost(len(first) * groups),
    )(me, lengths, x)
    later = pl.pallas_call(
        functools.partial(second_kernel, count=len(second), **sizes),
        out_shape=[half(second, 0)] * 2,
        in_specs=[SMEM] + [VMEM] * 2,
        out_specs=[VMEM] * 2,
        scratch_shapes=[pltpu.VMEM((len(second) * block, width), jnp.float32)],
        compiler_params=pltpu.CompilerParams(vmem_limit_bytes=32 << 20),
        cost_estimate=cost(len(second)),
    )(me, kept, done)
    return (mine, theirs), tuple(later), first, second


def total_of(refs, terms, height, size):
    parts = [refs[i][pl.ds(row, height), pl.ds(column, size)] for i, row, column in terms]
    return sum(parts[1:], parts[0])


def combine_kernel(*refs, plan, rows):
    outs = refs[len(refs) - len(plan):]
    for out, (size, atoms, extra) in zip(outs, plan):
        for place, terms in enumerate(atoms):
            out[pl.ds(place * rows, rows), :] = total_of(refs, terms, rows, size)
        if extra:
            out[pl.ds(len(atoms) * rows, EXTRA), :] = total_of(refs, extra, EXTRA, size)


def combine(arrays, plan, rows):
    used = sorted({t[0] for _, atoms, extra in plan for terms in atoms + [extra] for t in terms})
    where = {index: i for i, index in enumerate(used)}

    def local(terms):
        return [(where[i], row, column) for i, row, column in terms]

    plan = [(size, [local(terms) for terms in atoms], local(extra)) for size, atoms, extra in plan]
    return pl.pallas_call(
        functools.partial(combine_kernel, plan=plan, rows=rows),
        out_shape=[
            jax.ShapeDtypeStruct((len(atoms) * rows + EXTRA * bool(extra), size), jnp.float32)
            for size, atoms, extra in plan
        ],
        in_specs=[VMEM] * len(used),
        out_specs=[VMEM] * len(plan),
        compiler_params=pltpu.CompilerParams(vmem_limit_bytes=12 << 20),
    )(*[arrays[i] for i in used])


def finish_kernel(me_ref, *refs, plan, extra, rows, pack):
    cov_ref, mean_ref, count_ref = refs[-3:]
    width = cov_ref.shape[1]
    block = total_of(refs, extra, EXTRA, pack)
    lines = -(-width // pack)
    total = jnp.concatenate([block[i:i + 1] for i in range(lines)], axis=1)[:, :width]
    count = block[lines:lines + 1, 0:1]
    lane = lax.broadcasted_iota(jnp.int32, (rows, width), 1)
    row = lax.broadcasted_iota(jnp.int32, (rows, width), 0)
    own = jnp.sum(
        jnp.where(lane == row + me_ref[0] * rows, total, 0.0), axis=1, keepdims=True
    )
    mean = total / count
    mean_ref[...] = mean
    count_ref[...] = count
    for start, size, terms in plan:
        at = slice(start, start + size)
        second = total_of(refs, terms, rows, size) - own * mean[:, at]
        cov_ref[:, at] = second / (count - 1.0)


def solution(mesh):
    axes = ("grp", "mem")
    groups, members = mesh.shape["grp"], mesh.shape["mem"]
    devices = groups * members
    masks = exchange_masks(groups, members)

    def swap(value, mask):
        return lax.ppermute(value, axes, [(i, i ^ mask) for i in range(devices)])

    def body(features, lengths):
        width = features.shape[1]
        rows = width // devices
        portions = column_portions(masks, width)
        pack = portions[0][1]
        me = (lax.axis_index("grp") * members + lax.axis_index("mem")).reshape(1)
        early, late, first, second = grams(me, lengths[0], features, groups, members, pack)

        arrays = []
        tables = [{} for _ in portions]
        for keys, (mine, theirs) in ((first, early), (second, late)):
            arrays += [mine, swap(theirs, CORE)]
            sources = (len(arrays) - 2, len(arrays) - 1)
            relatives = [key * members + j for key in keys for j in range(0, members, 2)]
            for table, (start, _, _) in zip(tables, portions):
                for place, device in enumerate(relatives):
                    table[device] = [(i, place * rows, start) for i in sources]
        extra = [(i, len(first) * members // 2 * rows, 0) for i in (0, 1)]

        for step in range(len(masks)):
            if step == 0:
                batches = [lambda d: d & masks[0], lambda d: not d & masks[0]]
            else:
                batches = [lambda d: True]
            arrived = []
            for batch in batches:
                plan, sent = [], []
                for p, (_, size, order) in enumerate(portions):
                    mask = order[step]
                    chosen = [d for d in tables[p] if d & mask and batch(d)]
                    if chosen:
                        carried = extra if p == 0 else []
                        plan.append((size, [tables[p][d] for d in chosen], carried))
                        sent.append((p, mask, chosen))
                for (p, mask, chosen), item in zip(sent, plan):
                    message, = combine(arrays, [item], rows)
                    arrived.append((p, mask, chosen, swap(message, mask)))
            for p, mask, chosen, array in arrived:
                for place, device in enumerate(chosen):
                    terms = tables[p].pop(device)
                    tables[p][device ^ mask].append((len(arrays), place * rows, 0))
                if p == 0:
                    extra = extra + [(len(arrays), len(chosen) * rows, 0)]
                arrays.append(array)

        plan = [(start, size, table[0]) for table, (start, size, _) in zip(tables, portions)]
        used = sorted({t[0] for terms in [extra] + [terms for _, _, terms in plan] for t in terms})
        where = {index: i for i, index in enumerate(used)}
        plan = [(s, n, [(where[i], r, c) for i, r, c in terms]) for s, n, terms in plan]
        covariance, mean, count = pl.pallas_call(
            functools.partial(
                finish_kernel,
                plan=plan,
                extra=[(where[i], r, c) for i, r, c in extra],
                rows=rows,
                pack=pack,
            ),
            out_shape=[
                jax.ShapeDtypeStruct((rows, width), jnp.float32),
                jax.ShapeDtypeStruct((1, width), jnp.float32),
                jax.ShapeDtypeStruct((1, 1), jnp.float32),
            ],
            in_specs=[SMEM] + [VMEM] * len(used),
            out_specs=[VMEM] * 3,
            compiler_params=pltpu.CompilerParams(vmem_limit_bytes=12 << 20),
        )(me, *[arrays[i] for i in used])
        return count.reshape(1), mean.reshape(width), covariance

    return jax.shard_map(
        body,
        mesh=mesh,
        in_specs=(P(axes, None), P(axes, None)),
        out_specs=(P(), P(), P(axes, None)),
        check_vma=False,
    )
```

```python
import functools

import jax
import jax.numpy as jnp
from jax import lax
from jax.experimental import pallas as pl
from jax.experimental.pallas import tpu as pltpu
from jax.sharding import PartitionSpec as P

EXTRA = 8
SMEM = pl.BlockSpec(memory_space=pltpu.SMEM)
VMEM = pl.BlockSpec(memory_space=pltpu.VMEM)
HBM = pl.BlockSpec(memory_space=pltpu.HBM)


def member_masks(members):
    near = [1 << bit for bit in range(1, members.bit_length() - 1)]
    far = list(near)
    for i in range(0, len(far) - 1, 2):
        far[i], far[i + 1] = far[i + 1], far[i]
    return near, far


def member_order(masks):
    order = []
    for place in range(1 << len(masks)):
        member = 0
        for i, mask in enumerate(masks):
            if not place >> (len(masks) - 1 - i) & 1:
                member ^= mask
        order.append(member)
    return order


def dot_transposed(a, b):
    return lax.dot_general(a, b, (((0,), (0,)), ((), ())), preferred_element_type=jnp.float32)


def block_columns(group, key, block):
    return pl.ds(pl.multiple_of((group ^ key) * block, block), block)


def write_rows(outs, chunks, me, members, rows, keys):
    group, member = me // members, me % members
    core = me % 2
    block = members * rows
    orders = [member_order(masks) for masks in member_masks(members)]
    for out, other in zip(outs, (0, 1)):
        owner = core ^ other
        for c, chunk in enumerate(chunks):
            for i, (even, odd) in enumerate(zip(*orders)):
                relative = jnp.where(owner == 0, even, odd)
                start = ((member ^ other) ^ relative) * rows
                at = pl.ds((c * len(orders[0]) + i) * rows, rows)
                for n, key in enumerate(keys):
                    ref, row, column = chunk(owner, n)
                    source = pl.ds(pl.multiple_of(row + start, rows), rows)
                    out[at, block_columns(group, key, block)] = ref[source, pl.ds(column, block)]


def first_kernel(me_ref, len_hbm, x_hbm, mine_ref, theirs_ref, x_ref, acc_ref,
                 len_ref, sums_ref, sem, *, tile, keys, members, rows, pack):
    depth, width = x_hbm.shape
    block = members * rows
    tiles = depth // tile
    half_tiles = tiles // 2
    me = me_ref[0]
    group = me // members

    lengths = pltpu.make_async_copy(len_hbm, len_ref, sem.at[tiles])
    lengths.start()
    for i in range(tiles):
        part = pl.ds(i * tile, tile)
        for n, key in enumerate(keys):
            pltpu.make_async_copy(
                x_hbm.at[part, block_columns(group, key, block)],
                x_ref.at[part, pl.ds(n * block, block)],
                sem.at[i],
            ).start()
    lengths.wait()
    total = jnp.zeros((1, width), jnp.float32)
    for i in range(tiles):
        part = pl.ds(i * tile, tile)
        pltpu.make_async_copy(x_hbm.at[part], x_ref.at[part], sem.at[i]).wait()
        valid = len_ref[0, i // half_tiles] - (i % half_tiles) * tile

        @pl.when(valid < tile)
        def _():
            x = x_ref[part, :]
            position = lax.broadcasted_iota(jnp.int32, x.shape, 0)
            x_ref[part, :] = jnp.where(position < valid, x, jnp.zeros_like(x))

        total += jnp.sum(x_ref[part, :].astype(jnp.float32), axis=0, keepdims=True)
        product = dot_transposed(x_ref[part, 0:block], x_ref[part, :])
        if i:
            acc_ref[...] += product
        else:
            acc_ref[...] = product
    write_rows(
        (mine_ref, theirs_ref), [lambda owner, n: (acc_ref, 0, n * block)], me, members, rows, keys
    )
    for n, key in enumerate(keys):
        sums_ref[0:1, block_columns(group, key, block)] = total[:, n * block:(n + 1) * block]
    count = (len_ref[0, 0] + len_ref[0, 1]).astype(jnp.float32)
    for ref in (mine_ref, theirs_ref):
        ref[pl.ds(block // 2, EXTRA), :] = jnp.full((EXTRA, width), count)
        for line, start in enumerate(range(0, width, pack)):
            ref[pl.ds(block // 2 + line, 1), 0:pack] = sums_ref[0:1, start:start + pack]


def second_kernel(x_ref, acc_ref, *, block):
    acc_ref[...] = dot_transposed(x_ref[:, block:2 * block], x_ref[:, block:])


def third_kernel(me_ref, x_ref, first_ref, second_ref, after_ref, mine_ref, theirs_ref,
                 mine_rest_ref, theirs_rest_ref, acc_ref, *, keys, members, rows):
    block = members * rows

    def cut(n):
        return slice(n * block, (n + 1) * block)

    for n in (1, 2, 3):
        acc_ref[cut(n - 1), cut(0)] = first_ref[:, cut(n)].T
    acc_ref[cut(0), block:] = second_ref[...]
    for n in (2, 3):
        acc_ref[cut(n - 1), cut(1)] = second_ref[:, cut(n - 1)].T
    acc_ref[cut(1), 2 * block:] = dot_transposed(x_ref[:, cut(2)], x_ref[:, 2 * block:])
    acc_ref[cut(2), cut(3)] = dot_transposed(x_ref[:, cut(3)], x_ref[:, cut(3)])
    acc_ref[cut(2), cut(2)] = acc_ref[cut(1), cut(3)].T

    def step_one(owner, n):
        return acc_ref, owner * block, n * block

    def step_two(owner, n):
        return acc_ref, (1 - owner) * block, n * block

    def kept(owner, n):
        return acc_ref, 2 * block, n * block

    me = me_ref[0]
    write_rows((mine_ref, theirs_ref), [step_one], me, members, rows, keys)
    write_rows((mine_rest_ref, theirs_rest_ref), [step_two, kept], me, members, rows, keys)


def total_of(refs, terms, height, size):
    parts = [refs[i][pl.ds(row, height), pl.ds(column, size)] for i, row, column in terms]
    return sum(parts[1:], parts[0])


def sum_kernel(*refs, plan, size):
    out = refs[-1]
    at = 0
    for height, terms in plan:
        out[pl.ds(at, height), :] = total_of(refs, terms, height, size)
        at += height


def finish_kernel(me_ref, *refs, chains, extra, rows):
    cov_ref, mean_ref, count_ref = refs[-3:]
    width = cov_ref.shape[1]
    pack = width // len(chains)
    block = total_of(refs, extra, EXTRA, pack)
    total = jnp.concatenate([block[i:i + 1] for i in range(len(chains))], axis=1)
    count = block[len(chains):len(chains) + 1, 0:1]
    lane = lax.broadcasted_iota(jnp.int32, (rows, width), 1)
    row = lax.broadcasted_iota(jnp.int32, (rows, width), 0)
    own = jnp.sum(
        jnp.where(lane == row + me_ref[0] * rows, total, 0.0), axis=1, keepdims=True
    )
    mean = total / count
    mean_ref[...] = mean
    count_ref[...] = count
    for c, terms in enumerate(chains):
        at = slice(c * pack, (c + 1) * pack)
        second = total_of(refs, terms, rows, pack) - own * mean[:, at]
        cov_ref[:, at] = second / (count - 1.0)


def limit(mebibytes):
    return pltpu.CompilerParams(vmem_limit_bytes=mebibytes << 20)


def solution(mesh):
    axes = ("grp", "mem")
    groups, members = mesh.shape["grp"], mesh.shape["mem"]
    devices = groups * members
    keys = (3, 1, 2, 0)
    assert groups == len(keys)
    near, far = member_masks(members)
    steps = [(members, 2 * members), (2 * members, members), *zip(near, far)]

    def swap(value, masks):
        pairs = [(i, i ^ masks[i % 2]) for i in range(devices)]
        return lax.ppermute(value, axes, pairs)

    def body(features, lengths):
        depth, width = features.shape
        rows = width // devices
        block = members * rows
        half = block // 2
        pack = width // 2
        me = (lax.axis_index("grp") * members + lax.axis_index("mem")).reshape(1)

        def f32(height, size=width):
            return jax.ShapeDtypeStruct((height, size), jnp.float32)

        def cost(blocks):
            return pl.CostEstimate(
                flops=2 * depth * block * block * blocks,
                bytes_accessed=depth * width * 2,
                transcendentals=0,
            )

        tile = depth // 4
        sizes = dict(keys=keys, members=members, rows=rows)
        mine, theirs, x, acc = pl.pallas_call(
            functools.partial(first_kernel, tile=tile, pack=pack, **sizes),
            out_shape=[f32(half + EXTRA)] * 2
            + [jax.ShapeDtypeStruct(features.shape, features.dtype), f32(block)],
            in_specs=[SMEM, HBM, HBM],
            out_specs=[VMEM] * 4,
            scratch_shapes=[
                pltpu.SMEM(lengths.shape, jnp.int32),
                pltpu.VMEM((EXTRA, width), jnp.float32),
                pltpu.SemaphoreType.DMA((depth // tile + 1,)),
            ],
            compiler_params=limit(40),
            cost_estimate=cost(4),
        )(me, lengths, features)
        arrays, narrow = [], []
        acc_next = pl.pallas_call(
            functools.partial(second_kernel, block=block),
            out_shape=jax.ShapeDtypeStruct((block, width - block), jnp.float32),
            in_specs=[VMEM],
            out_specs=VMEM,
            compiler_params=limit(32),
            cost_estimate=cost(3),
        )(x)

        def localise(used, terms, start):
            return [(used.index(i), row, 0 if narrow[i] else start) for i, row in terms]

        def total(plan, start, size, after=()):
            used = sorted({i for _, terms in plan for i, _ in terms}.union(after))
            plan = [(height, localise(used, terms, start)) for height, terms in plan]
            return pl.pallas_call(
                functools.partial(sum_kernel, plan=plan, size=size),
                out_shape=f32(sum(height for height, _ in plan), size),
                in_specs=[VMEM] * len(used),
                out_specs=VMEM,
                compiler_params=limit(12),
                cost_estimate=pl.CostEstimate(flops=1, bytes_accessed=1, transcendentals=0),
            )(*[arrays[i] for i in used])

        def put(array, wide=True):
            arrays.append(array)
            narrow.append(not wide)
            return len(arrays) - 1

        one, one_in = put(mine), put(swap(theirs, (1, 1)))
        extra = [(one, half), (one_in, half)]
        message = total([(half, [(one, 0), (one_in, 0)]), (EXTRA, extra)], 0, width)
        one_next = put(swap(message, steps[0]))
        mine, theirs, mine_rest, theirs_rest = pl.pallas_call(
            functools.partial(third_kernel, **sizes),
            out_shape=[f32(half)] * 2 + [f32(2 * half)] * 2,
            in_specs=[SMEM] + [VMEM] * 4,
            out_specs=[VMEM] * 4,
            scratch_shapes=[pltpu.VMEM((3 * block, width), jnp.float32)],
            compiler_params=limit(32),
            cost_estimate=cost(3),
        )(me, x, acc, acc_next, message)
        two, two_in = put(mine), put(swap(theirs, (1, 1)))
        rest, rest_in = put(mine_rest), put(swap(theirs_rest, (1, 1)))
        extra.append((one_next, half))

        starts = range(0, width, pack)
        two_next = [
            put(swap(total([(half, [(two, 0), (two_in, 0)])], start, pack), steps[0]), False)
            for start in starts
        ]
        chains = []
        for start, two_out in zip(starts, two_next):
            carried = [] if start else [(EXTRA, extra)]
            message = total(
                [(half, [(rest, 0), (rest_in, 0), (one_next, 0)])] + carried, start, pack, [two_out]
            )
            added = put(swap(message, steps[1]), False)
            chains.append([(rest, half), (rest_in, half), (two_out, 0), (added, 0)])
            if not start:
                extra = extra + [(added, half)]
        height = half
        for masks in steps[2:]:
            height //= 2
            for c, start in enumerate(starts):
                carried = [] if start else [(EXTRA, extra)]
                message = total([(height, chains[c])] + carried, start, pack)
                added = put(swap(message, masks), False)
                chains[c] = [(i, row + height) for i, row in chains[c]] + [(added, 0)]
                if not start:
                    extra = extra + [(added, height)]

        used = sorted({i for terms in chains + [extra] for i, _ in terms})
        covariance, mean, count = pl.pallas_call(
            functools.partial(
                finish_kernel,
                chains=[localise(used, terms, start) for terms, start in zip(chains, starts)],
                extra=localise(used, extra, 0),
                rows=rows,
            ),
            out_shape=[f32(rows), f32(1), jax.ShapeDtypeStruct((1, 1), jnp.float32)],
            in_specs=[SMEM] + [VMEM] * len(used),
            out_specs=[VMEM] * 3,
            compiler_params=limit(12),
            cost_estimate=pl.CostEstimate(flops=1, bytes_accessed=1, transcendentals=0),
        )(me, *[arrays[i] for i in used])
        return count.reshape(1), mean.reshape(width), covariance

    return jax.shard_map(
        body,
        mesh=mesh,
        in_specs=(P(axes, None), P(axes, None)),
        out_specs=(P(), P(), P(axes, None)),
        check_vma=False,
    )
```

```python
import functools

import jax
import jax.numpy as jnp
from jax import lax
from jax.experimental import pallas as pl
from jax.experimental.pallas import tpu as pltpu
from jax.sharding import PartitionSpec as P

LANES = 128
EXTRA = 8
CHAINS = 2
SMEM = pl.BlockSpec(memory_space=pltpu.SMEM)
VMEM = pl.BlockSpec(memory_space=pltpu.VMEM)
HBM = pl.BlockSpec(memory_space=pltpu.HBM)


def member_masks(members):
    near = [1 << bit for bit in range(1, members.bit_length() - 1)]
    far = list(near)
    for i in range(0, len(far) - 1, 2):
        far[i], far[i + 1] = far[i + 1], far[i]
    return near, far


def member_order(masks):
    order = []
    for place in range(1 << len(masks)):
        member = 0
        for i, mask in enumerate(masks):
            if not place >> (len(masks) - 1 - i) & 1:
                member ^= mask
        order.append(member)
    return order


def dot_transposed(a, b):
    return lax.dot_general(a, b, (((0,), (0,)), ((), ())), preferred_element_type=jnp.float32)


def block_columns(group, key, block):
    return pl.ds(pl.multiple_of((group ^ key) * block, block), block)


def write_rows(outs, chunks, me, members, rows, keys):
    group, member = me // members, me % members
    core = me % 2
    block = members * rows
    orders = [member_order(masks) for masks in member_masks(members)]
    for out, other in zip(outs, (0, 1)):
        owner = core ^ other
        for c, chunk in enumerate(chunks):
            for i, (even, odd) in enumerate(zip(*orders)):
                relative = jnp.where(owner == 0, even, odd)
                start = ((member ^ other) ^ relative) * rows
                place = (c * len(orders[0]) + i) * rows
                target = out
                if isinstance(out, tuple):
                    target = out[place // out[0].shape[0]]
                    place %= out[0].shape[0]
                at = pl.ds(place, rows)
                for n, key in enumerate(keys):
                    ref, row, column = chunk(owner, n)
                    source = pl.ds(pl.multiple_of(row + start, rows), rows)
                    target[at, block_columns(group, key, block)] = ref[source, pl.ds(column, block)]


def first_kernel(me_ref, len_hbm, x_hbm, mine_ref, theirs_ref, x_ref, acc_ref,
                 len_ref, sums_ref, sem, *, tile, keys, members, rows, pack):
    depth, width = x_hbm.shape
    block = members * rows
    tiles = depth // tile
    half_tiles = tiles // 2
    me = me_ref[0]
    group = me // members

    lengths = pltpu.make_async_copy(len_hbm, len_ref, sem.at[tiles])
    lengths.start()
    for i in range(tiles):
        part = pl.ds(i * tile, tile)
        for n, key in enumerate(keys):
            pltpu.make_async_copy(
                x_hbm.at[part, block_columns(group, key, block)],
                x_ref.at[part, pl.ds(n * block, block)],
                sem.at[i],
            ).start()
    lengths.wait()
    total = jnp.zeros((1, width), jnp.float32)
    for i in range(tiles):
        part = pl.ds(i * tile, tile)
        pltpu.make_async_copy(x_hbm.at[part], x_ref.at[part], sem.at[i]).wait()
        valid = len_ref[0, i // half_tiles] - (i % half_tiles) * tile

        @pl.when(valid < tile)
        def _():
            x = x_ref[part, :]
            position = lax.broadcasted_iota(jnp.int32, x.shape, 0)
            x_ref[part, :] = jnp.where(position < valid, x, jnp.zeros_like(x))

        total += jnp.sum(x_ref[part, :].astype(jnp.float32), axis=0, keepdims=True)
        product = dot_transposed(x_ref[part, 0:block], x_ref[part, :])
        if i:
            acc_ref[...] += product
        else:
            acc_ref[...] = product
    write_rows(
        (mine_ref, theirs_ref), [lambda owner, n: (acc_ref, 0, n * block)], me, members, rows, keys
    )
    for n, key in enumerate(keys):
        sums_ref[0:1, block_columns(group, key, block)] = total[:, n * block:(n + 1) * block]
    count = (len_ref[0, 0] + len_ref[0, 1]).astype(jnp.float32)
    for ref in (mine_ref, theirs_ref):
        ref[pl.ds(block // 2, EXTRA), :] = jnp.full((EXTRA, width), count)
        for line, start in enumerate(range(0, width, pack)):
            size = min(pack, width - start)
            ref[pl.ds(block // 2 + line, 1), 0:size] = sums_ref[0:1, start:start + size]


def second_kernel(x_ref, acc_ref, *, block):
    acc_ref[...] = dot_transposed(x_ref[:, block:2 * block], x_ref[:, block:])


def third_kernel(me_ref, x_ref, first_ref, second_ref, after_ref, mine_ref, theirs_ref,
                 theirs_later_ref, mine_next_ref, theirs_next_ref, mine_last_ref, theirs_last_ref, acc_ref,
                 *, keys, members, rows):
    block = members * rows

    def cut(n):
        return slice(n * block, (n + 1) * block)

    for n in (1, 2, 3):
        acc_ref[cut(n - 1), cut(0)] = first_ref[:, cut(n)].T
    acc_ref[cut(0), block:] = second_ref[...]
    for n in (2, 3):
        acc_ref[cut(n - 1), cut(1)] = second_ref[:, cut(n - 1)].T
    acc_ref[cut(1), 2 * block:] = dot_transposed(x_ref[:, cut(2)], x_ref[:, 2 * block:])
    acc_ref[cut(2), cut(3)] = dot_transposed(x_ref[:, cut(3)], x_ref[:, cut(3)])
    acc_ref[cut(2), cut(2)] = acc_ref[cut(1), cut(3)].T

    def step_one(owner, n):
        return acc_ref, owner * block, n * block

    def step_two(owner, n):
        return acc_ref, (1 - owner) * block, n * block

    def kept(owner, n):
        return acc_ref, 2 * block, n * block

    me = me_ref[0]
    write_rows((mine_ref, (theirs_ref, theirs_later_ref)), [step_one], me, members, rows, keys)
    write_rows((mine_next_ref, theirs_next_ref), [step_two], me, members, rows, keys)
    write_rows((mine_last_ref, theirs_last_ref), [kept], me, members, rows, keys)


def total_of(refs, terms, height, size):
    parts = [refs[i][pl.ds(row, height), pl.ds(column, size)] for i, row, column in terms]
    return sum(parts[1:], parts[0])


def sum_kernel(*refs, plan, size):
    out = refs[-1]
    at = 0
    for height, terms in plan:
        out[pl.ds(at, height), :] = total_of(refs, terms, height, size)
        at += height


def finish_kernel(me_ref, *refs, chains, ranges, extra, rows):
    cov_ref, mean_ref, count_ref = refs[-3:]
    width = cov_ref.shape[1]
    pack = ranges[0][1]
    lines = -(-width // pack)
    block = total_of(refs, extra, EXTRA, pack)
    total = jnp.concatenate([block[i:i + 1] for i in range(lines)], axis=1)[:, :width]
    count = block[lines:lines + 1, 0:1]
    lane = lax.broadcasted_iota(jnp.int32, (rows, width), 1)
    row = lax.broadcasted_iota(jnp.int32, (rows, width), 0)
    own = jnp.sum(
        jnp.where(lane == row + me_ref[0] * rows, total, 0.0), axis=1, keepdims=True
    )
    mean = total / count
    mean_ref[...] = mean
    count_ref[...] = count
    for (start, size), terms in zip(ranges, chains):
        second = total_of(refs, terms, rows, size) - own * mean[:, start:start + size]
        cov_ref[:, start:start + size] = second / (count - 1.0)


def column_ranges(width, parts):
    tiles, ranges, start = width // LANES, [], 0
    for i in range(parts):
        size = (tiles + parts - 1 - i) // parts * LANES
        ranges.append((start, size))
        start += size
    return ranges


def limit(mebibytes):
    return pltpu.CompilerParams(vmem_limit_bytes=mebibytes << 20)


def solution(mesh):
    axes = ("grp", "mem")
    groups, members = mesh.shape["grp"], mesh.shape["mem"]
    devices = groups * members
    keys = (3, 1, 2, 0)
    assert groups == len(keys)
    near, far = member_masks(members)
    steps = [(members, 2 * members), (2 * members, members), *zip(near, far)]

    def swap(value, masks):
        pairs = [(i, i ^ masks[i % 2]) for i in range(devices)]
        return lax.ppermute(value, axes, pairs)

    def body(features, lengths):
        depth, width = features.shape
        rows = width // devices
        block = members * rows
        half = block // 2
        ranges = column_ranges(width, CHAINS)
        pack = ranges[0][1]
        me = (lax.axis_index("grp") * members + lax.axis_index("mem")).reshape(1)

        def f32(height, size=width):
            return jax.ShapeDtypeStruct((height, size), jnp.float32)

        def cost(blocks):
            return pl.CostEstimate(
                flops=2 * depth * block * block * blocks,
                bytes_accessed=depth * width * 2,
                transcendentals=0,
            )

        tile = depth // 4
        sizes = dict(keys=keys, members=members, rows=rows)
        mine, theirs, x, acc = pl.pallas_call(
            functools.partial(first_kernel, tile=tile, pack=pack, **sizes),
            out_shape=[f32(half + EXTRA)] * 2
            + [jax.ShapeDtypeStruct(features.shape, features.dtype), f32(block)],
            in_specs=[SMEM, HBM, HBM],
            out_specs=[VMEM] * 4,
            scratch_shapes=[
                pltpu.SMEM(lengths.shape, jnp.int32),
                pltpu.VMEM((EXTRA, width), jnp.float32),
                pltpu.SemaphoreType.DMA((depth // tile + 1,)),
            ],
            compiler_params=limit(40),
            cost_estimate=cost(4),
        )(me, lengths, features)
        arrays, narrow = [], []
        acc_next = pl.pallas_call(
            functools.partial(second_kernel, block=block),
            out_shape=jax.ShapeDtypeStruct((block, width - block), jnp.float32),
            in_specs=[VMEM],
            out_specs=VMEM,
            compiler_params=limit(32),
            cost_estimate=cost(3),
        )(x)

        def localise(used, terms, start):
            return [(used.index(i), row, 0 if narrow[i] else start) for i, row in terms]

        def total(plan, start, size, after=()):
            used = sorted({i for _, terms in plan for i, _ in terms}.union(after))
            plan = [(height, localise(used, terms, start)) for height, terms in plan]
            return pl.pallas_call(
                functools.partial(sum_kernel, plan=plan, size=size),
                out_shape=f32(sum(height for height, _ in plan), size),
                in_specs=[VMEM] * len(used),
                out_specs=VMEM,
                compiler_params=limit(12),
                cost_estimate=pl.CostEstimate(flops=1, bytes_accessed=1, transcendentals=0),
            )(*[arrays[i] for i in used])

        def put(array, wide=True):
            arrays.append(array)
            narrow.append(not wide)
            return len(arrays) - 1

        one, one_in = put(mine), put(swap(theirs, (1, 1)))
        extra = [(one, half), (one_in, half)]
        message = total([(half, [(one, 0), (one_in, 0)]), (EXTRA, extra)], 0, width)
        one_next = put(swap(message, steps[0]))
        mine, theirs, theirs_later, mine_next, theirs_next, mine_last, theirs_last = pl.pallas_call(
            functools.partial(third_kernel, **sizes),
            out_shape=[f32(half)] + [f32(half // 2)] * 2 + [f32(half)] * 4,
            in_specs=[SMEM] + [VMEM] * 4,
            out_specs=[VMEM] * 7,
            scratch_shapes=[pltpu.VMEM((3 * block, width), jnp.float32)],
            compiler_params=limit(32),
            cost_estimate=cost(3),
        )(me, x, acc, acc_next, message)
        two, two_in = put(mine), [put(swap(part, (1, 1))) for part in (theirs, theirs_later)]
        after, after_in = put(mine_next), put(swap(theirs_next, (1, 1)))
        last, last_in = put(mine_last), put(swap(theirs_last, (1, 1)))
        extra.append((one_next, half))
        both = [(half // 2, [(two, i * half // 2), (other, 0)]) for i, other in enumerate(two_in)]
        two_next = [
            put(swap(total(both, *columns), steps[0]), False) for columns in ranges
        ]
        chains = []
        for (start, size), two_out in zip(ranges, two_next):
            carried = [] if start else [(EXTRA, extra)]
            message = total(
                [(half, [(after, 0), (after_in, 0), (one_next, 0)])] + carried, start, size, [two_out]
            )
            added = put(swap(message, steps[1]), False)
            chains.append([(last, 0), (last_in, 0), (two_out, 0), (added, 0)])
            if not start:
                extra = extra + [(added, half)]
        height = half
        for masks in steps[2:]:
            height //= 2
            for c, (start, size) in enumerate(ranges):
                carried = [] if start else [(EXTRA, extra)]
                message = total([(height, chains[c])] + carried, start, size)
                added = put(swap(message, masks), False)
                chains[c] = [(i, row + height) for i, row in chains[c]] + [(added, 0)]
                if not start:
                    extra = extra + [(added, height)]

        used = sorted({i for terms in chains + [extra] for i, _ in terms})
        covariance, mean, count = pl.pallas_call(
            functools.partial(
                finish_kernel,
                chains=[localise(used, terms, start) for terms, (start, _) in zip(chains, ranges)],
                ranges=ranges,
                extra=localise(used, extra, 0),
                rows=rows,
            ),
            out_shape=[f32(rows), f32(1), jax.ShapeDtypeStruct((1, 1), jnp.float32)],
            in_specs=[SMEM] + [VMEM] * len(used),
            out_specs=[VMEM] * 3,
            compiler_params=limit(12),
            cost_estimate=pl.CostEstimate(flops=1, bytes_accessed=1, transcendentals=0),
        )(me, *[arrays[i] for i in used])
        return count.reshape(1), mean.reshape(width), covariance

    return jax.shard_map(
        body,
        mesh=mesh,
        in_specs=(P(axes, None), P(axes, None)),
        out_specs=(P(), P(), P(axes, None)),
        check_vma=False,
    )
```

```python
import functools

import jax
import jax.numpy as jnp
from jax import lax
from jax.experimental import pallas as pl
from jax.experimental.pallas import tpu as pltpu
from jax.sharding import PartitionSpec as P

LANES = 128
EXTRA = 8
CHAINS = 2
SMEM = pl.BlockSpec(memory_space=pltpu.SMEM)
VMEM = pl.BlockSpec(memory_space=pltpu.VMEM)
HBM = pl.BlockSpec(memory_space=pltpu.HBM)


def member_masks(members):
    return [1 << bit for bit in range(1, members.bit_length() - 1)]


def member_order(masks):
    order = []
    for place in range(1 << len(masks)):
        member = 0
        for i, mask in enumerate(masks):
            if not place >> (len(masks) - 1 - i) & 1:
                member ^= mask
        order.append(member)
    return order


def dot_transposed(a, b):
    return lax.dot_general(a, b, (((0,), (0,)), ((), ())), preferred_element_type=jnp.float32)


def block_columns(group, key, block):
    return pl.ds(pl.multiple_of((group ^ key) * block, block), block)


def write_rows(outs, chunks, me, members, rows, keys):
    group, member = me // members, me % members
    core = me % 2
    block = members * rows
    order = member_order(member_masks(members))
    for out, other in zip(outs, (0, 1)):
        owner = core ^ other
        for c, chunk in enumerate(chunks):
            for i, relative in enumerate(order):
                start = (member ^ other ^ relative) * rows
                place = (c * len(order) + i) * rows
                target = out
                if isinstance(out, tuple):
                    target = out[place // out[0].shape[0]]
                    place %= out[0].shape[0]
                at = pl.ds(place, rows)
                for n, key in enumerate(keys):
                    ref, row, column = chunk(owner, n)
                    source = pl.ds(pl.multiple_of(row + start, rows), rows)
                    target[at, block_columns(group, key, block)] = ref[source, pl.ds(column, block)]


def first_kernel(me_ref, len_hbm, x_hbm, mine_ref, theirs_ref, x_ref, acc_ref,
                 len_ref, sums_ref, sem, *, tile, keys, members, rows, pack):
    depth, width = x_hbm.shape
    block = members * rows
    tiles = depth // tile
    half_tiles = tiles // 2
    me = me_ref[0]
    group = me // members

    lengths = pltpu.make_async_copy(len_hbm, len_ref, sem.at[tiles])
    lengths.start()
    for i in range(tiles):
        part = pl.ds(i * tile, tile)
        for n, key in enumerate(keys):
            pltpu.make_async_copy(
                x_hbm.at[part, block_columns(group, key, block)],
                x_ref.at[part, pl.ds(n * block, block)],
                sem.at[i],
            ).start()
    lengths.wait()
    total = jnp.zeros((1, width), jnp.float32)
    for i in range(tiles):
        part = pl.ds(i * tile, tile)
        pltpu.make_async_copy(x_hbm.at[part], x_ref.at[part], sem.at[i]).wait()
        valid = len_ref[0, i // half_tiles] - (i % half_tiles) * tile

        @pl.when(valid < tile)
        def _():
            x = x_ref[part, :]
            position = lax.broadcasted_iota(jnp.int32, x.shape, 0)
            x_ref[part, :] = jnp.where(position < valid, x, jnp.zeros_like(x))

        total += jnp.sum(x_ref[part, :].astype(jnp.float32), axis=0, keepdims=True)
        product = dot_transposed(x_ref[part, 0:block], x_ref[part, :])
        if i:
            acc_ref[...] += product
        else:
            acc_ref[...] = product
    write_rows(
        (mine_ref, theirs_ref), [lambda owner, n: (acc_ref, 0, n * block)], me, members, rows, keys
    )
    for n, key in enumerate(keys):
        sums_ref[0:1, block_columns(group, key, block)] = total[:, n * block:(n + 1) * block]
    count = (len_ref[0, 0] + len_ref[0, 1]).astype(jnp.float32)
    for ref in (mine_ref, theirs_ref):
        ref[pl.ds(block // 2, EXTRA), :] = jnp.full((EXTRA, width), count)
        for line, start in enumerate(range(0, width, pack)):
            size = min(pack, width - start)
            ref[pl.ds(block // 2 + line, 1), 0:size] = sums_ref[0:1, start:start + size]


def second_kernel(x_ref, acc_ref, *, block):
    acc_ref[...] = dot_transposed(x_ref[:, block:2 * block], x_ref[:, block:])


def third_kernel(me_ref, x_ref, first_ref, second_ref, after_ref, mine_ref, theirs_ref,
                 theirs_later_ref, mine_next_ref, theirs_next_ref, mine_last_ref, theirs_last_ref, acc_ref,
                 *, keys, members, rows):
    block = members * rows

    def cut(n):
        return slice(n * block, (n + 1) * block)

    for n in (1, 2, 3):
        acc_ref[cut(n - 1), cut(0)] = first_ref[:, cut(n)].T
    acc_ref[cut(0), block:] = second_ref[...]
    for n in (2, 3):
        acc_ref[cut(n - 1), cut(1)] = second_ref[:, cut(n - 1)].T
    acc_ref[cut(1), 2 * block:] = dot_transposed(x_ref[:, cut(2)], x_ref[:, 2 * block:])
    acc_ref[cut(2), cut(3)] = dot_transposed(x_ref[:, cut(3)], x_ref[:, cut(3)])
    acc_ref[cut(2), cut(2)] = acc_ref[cut(1), cut(3)].T

    def step_one(owner, n):
        return acc_ref, owner * block, n * block

    def step_two(owner, n):
        return acc_ref, (1 - owner) * block, n * block

    def kept(owner, n):
        return acc_ref, 2 * block, n * block

    me = me_ref[0]
    write_rows((mine_ref, (theirs_ref, theirs_later_ref)), [step_one], me, members, rows, keys)
    write_rows((mine_next_ref, theirs_next_ref), [step_two], me, members, rows, keys)
    write_rows((mine_last_ref, theirs_last_ref), [kept], me, members, rows, keys)


def total_of(refs, terms, height, size):
    parts = [refs[i][pl.ds(row, height), pl.ds(column, size)] for i, row, column in terms]
    return sum(parts[1:], parts[0])


def sum_kernel(*refs, plan, size):
    out = refs[-1]
    at = 0
    for height, terms in plan:
        out[pl.ds(at, height), :] = total_of(refs, terms, height, size)
        at += height


def finish_kernel(me_ref, *refs, chains, ranges, extra, rows):
    cov_ref, mean_ref, count_ref = refs[-3:]
    width = cov_ref.shape[1]
    pack = ranges[0][1]
    lines = -(-width // pack)
    block = total_of(refs, extra, EXTRA, pack)
    total = jnp.concatenate([block[i:i + 1] for i in range(lines)], axis=1)[:, :width]
    count = block[lines:lines + 1, 0:1]
    lane = lax.broadcasted_iota(jnp.int32, (rows, width), 1)
    row = lax.broadcasted_iota(jnp.int32, (rows, width), 0)
    own = jnp.sum(
        jnp.where(lane == row + me_ref[0] * rows, total, 0.0), axis=1, keepdims=True
    )
    mean = total / count
    mean_ref[...] = mean
    count_ref[...] = count
    for (start, size), terms in zip(ranges, chains):
        second = total_of(refs, terms, rows, size) - own * mean[:, start:start + size]
        cov_ref[:, start:start + size] = second / (count - 1.0)


def column_ranges(width, parts):
    tiles, ranges, start = width // LANES, [], 0
    for i in range(parts):
        size = (tiles + parts - 1 - i) // parts * LANES
        ranges.append((start, size))
        start += size
    return ranges


def limit(mebibytes):
    return pltpu.CompilerParams(vmem_limit_bytes=mebibytes << 20)


def solution(mesh):
    axes = ("grp", "mem")
    groups, members = mesh.shape["grp"], mesh.shape["mem"]
    devices = groups * members
    keys = (3, 1, 2, 0)
    assert groups == len(keys)
    steps = [(members, 2 * members), (2 * members, members)]
    steps += [(mask, mask) for mask in member_masks(members)]

    def swap(value, masks):
        pairs = [(i, i ^ masks[i % 2]) for i in range(devices)]
        return lax.ppermute(value, axes, pairs)

    def body(features, lengths):
        depth, width = features.shape
        rows = width // devices
        block = members * rows
        half = block // 2
        ranges = column_ranges(width, CHAINS)
        pack = ranges[0][1]
        me = (lax.axis_index("grp") * members + lax.axis_index("mem")).reshape(1)

        def f32(height, size=width):
            return jax.ShapeDtypeStruct((height, size), jnp.float32)

        def cost(blocks):
            return pl.CostEstimate(
                flops=2 * depth * block * block * blocks,
                bytes_accessed=depth * width * 2,
                transcendentals=0,
            )

        tile = depth // 4
        sizes = dict(keys=keys, members=members, rows=rows)
        mine, theirs, x, acc = pl.pallas_call(
            functools.partial(first_kernel, tile=tile, pack=pack, **sizes),
            out_shape=[f32(half + EXTRA)] * 2
            + [jax.ShapeDtypeStruct(features.shape, features.dtype), f32(block)],
            in_specs=[SMEM, HBM, HBM],
            out_specs=[VMEM] * 4,
            scratch_shapes=[
                pltpu.SMEM(lengths.shape, jnp.int32),
                pltpu.VMEM((EXTRA, width), jnp.float32),
                pltpu.SemaphoreType.DMA((depth // tile + 1,)),
            ],
            compiler_params=limit(40),
            cost_estimate=cost(4),
        )(me, lengths, features)
        arrays, narrow = [], []
        acc_next = pl.pallas_call(
            functools.partial(second_kernel, block=block),
            out_shape=jax.ShapeDtypeStruct((block, width - block), jnp.float32),
            in_specs=[VMEM],
            out_specs=VMEM,
            compiler_params=limit(32),
            cost_estimate=cost(3),
        )(x)

        def localise(used, terms, start):
            return [(used.index(i), row, 0 if narrow[i] else start) for i, row in terms]

        def total(plan, start, size, after=()):
            used = sorted({i for _, terms in plan for i, _ in terms}.union(after))
            plan = [(height, localise(used, terms, start)) for height, terms in plan]
            return pl.pallas_call(
                functools.partial(sum_kernel, plan=plan, size=size),
                out_shape=f32(sum(height for height, _ in plan), size),
                in_specs=[VMEM] * len(used),
                out_specs=VMEM,
                compiler_params=limit(12),
                cost_estimate=pl.CostEstimate(flops=1, bytes_accessed=1, transcendentals=0),
            )(*[arrays[i] for i in used])

        def put(array, wide=True):
            arrays.append(array)
            narrow.append(not wide)
            return len(arrays) - 1

        one, one_in = put(mine), put(swap(theirs, (1, 1)))
        extra = [(one, half), (one_in, half)]
        message = total([(half, [(one, 0), (one_in, 0)]), (EXTRA, extra)], 0, width)
        one_next = put(swap(message, steps[0]))
        mine, theirs, theirs_later, mine_next, theirs_next, mine_last, theirs_last = pl.pallas_call(
            functools.partial(third_kernel, **sizes),
            out_shape=[f32(half)] + [f32(half // 2)] * 2 + [f32(half)] * 4,
            in_specs=[SMEM] + [VMEM] * 4,
            out_specs=[VMEM] * 7,
            scratch_shapes=[pltpu.VMEM((3 * block, width), jnp.float32)],
            compiler_params=limit(32),
            cost_estimate=cost(3),
        )(me, x, acc, acc_next, message)
        two, two_in = put(mine), [put(swap(part, (1, 1))) for part in (theirs, theirs_later)]
        after, after_in = put(mine_next), put(swap(theirs_next, (1, 1)))
        last, last_in = put(mine_last), put(swap(theirs_last, (1, 1)))
        extra.append((one_next, half))
        both = [(half // 2, [(two, i * half // 2), (other, 0)]) for i, other in enumerate(two_in)]
        two_sent = [put(total(both, *columns), False) for columns in ranges]
        two_next = [put(swap(arrays[i], steps[0]), False) for i in two_sent]
        chains = []
        for (start, size), two_out in zip(ranges, two_next):
            carried = [] if start else [(EXTRA, extra)]
            message = total(
                [(half, [(after, 0), (after_in, 0), (one_next, 0)])] + carried, start, size, two_next[:1] if start else two_sent
            )
            added = put(swap(message, steps[1]), False)
            chains.append([(last, 0), (last_in, 0), (two_out, 0), (added, 0)])
            if not start:
                extra = extra + [(added, half)]
        height = half
        for masks in steps[2:]:
            height //= 2
            for c, (start, size) in enumerate(ranges):
                carried = [] if start else [(EXTRA, extra)]
                message = total([(height, chains[c])] + carried, start, size)
                added = put(swap(message, masks), False)
                chains[c] = [(i, row + height) for i, row in chains[c]] + [(added, 0)]
                if not start:
                    extra = extra + [(added, height)]

        used = sorted({i for terms in chains + [extra] for i, _ in terms})
        covariance, mean, count = pl.pallas_call(
            functools.partial(
                finish_kernel,
                chains=[localise(used, terms, start) for terms, (start, _) in zip(chains, ranges)],
                ranges=ranges,
                extra=localise(used, extra, 0),
                rows=rows,
            ),
            out_shape=[f32(rows), f32(1), jax.ShapeDtypeStruct((1, 1), jnp.float32)],
            in_specs=[SMEM] + [VMEM] * len(used),
            out_specs=[VMEM] * 3,
            compiler_params=limit(12),
            cost_estimate=pl.CostEstimate(flops=1, bytes_accessed=1, transcendentals=0),
        )(me, *[arrays[i] for i in used])
        return count.reshape(1), mean.reshape(width), covariance

    return jax.shard_map(
        body,
        mesh=mesh,
        in_specs=(P(axes, None), P(axes, None)),
        out_specs=(P(), P(), P(axes, None)),
        check_vma=False,
    )
```

```python
import functools

import jax
import jax.numpy as jnp
from jax import lax
from jax.experimental import pallas as pl
from jax.experimental.pallas import tpu as pltpu
from jax.sharding import PartitionSpec as P

LANES = 128
EXTRA = 8
CHAINS = 2
SMEM = pl.BlockSpec(memory_space=pltpu.SMEM)
VMEM = pl.BlockSpec(memory_space=pltpu.VMEM)
HBM = pl.BlockSpec(memory_space=pltpu.HBM)


def member_masks(members):
    near = [1 << bit for bit in range(1, members.bit_length() - 1)]
    far = list(near)
    for i in range(0, len(far) - 1, 2):
        far[i], far[i + 1] = far[i + 1], far[i]
    return near, far


def member_order(masks):
    order = []
    for place in range(1 << len(masks)):
        member = 0
        for i, mask in enumerate(masks):
            if not place >> (len(masks) - 1 - i) & 1:
                member ^= mask
        order.append(member)
    return order


def dot_transposed(a, b):
    return lax.dot_general(a, b, (((0,), (0,)), ((), ())), preferred_element_type=jnp.float32)


def block_columns(group, key, block):
    return pl.ds(pl.multiple_of((group ^ key) * block, block), block)


def write_rows(outs, chunks, me, members, rows, keys, pack):
    group, member = me // members, me % members
    core = me % 2
    block = members * rows
    orders = [member_order(masks) for masks in member_masks(members)]
    for out, other in zip(outs, (0, 1)):
        owner = core ^ other
        lanes = [owner ^ ((group ^ key) * block // pack) for key in keys]
        for c, chunk in enumerate(chunks):
            for i, (even, odd) in enumerate(zip(*orders)):
                place = (c * len(orders[0]) + i) * rows
                target = out
                if isinstance(out, tuple):
                    target = out[place // out[0].shape[0]]
                    place %= out[0].shape[0]
                at = pl.ds(place, rows)
                for n, key in enumerate(keys):
                    relative = jnp.where(lanes[n] == 0, even, odd)
                    start = ((member ^ other) ^ relative) * rows
                    ref, row, column = chunk(owner, n)
                    source = pl.ds(pl.multiple_of(row + start, rows), rows)
                    target[at, block_columns(group, key, block)] = ref[source, pl.ds(column, block)]


def first_kernel(me_ref, len_hbm, x_hbm, mine_ref, theirs_ref, x_ref, acc_ref,
                 len_ref, sums_ref, sem, *, tile, keys, members, rows, pack):
    depth, width = x_hbm.shape
    block = members * rows
    tiles = depth // tile
    half_tiles = tiles // 2
    me = me_ref[0]
    group = me // members

    lengths = pltpu.make_async_copy(len_hbm, len_ref, sem.at[tiles])
    lengths.start()
    for i in range(tiles):
        part = pl.ds(i * tile, tile)
        for n, key in enumerate(keys):
            pltpu.make_async_copy(
                x_hbm.at[part, block_columns(group, key, block)],
                x_ref.at[part, pl.ds(n * block, block)],
                sem.at[i],
            ).start()
    lengths.wait()
    total = jnp.zeros((1, width), jnp.float32)
    for i in range(tiles):
        part = pl.ds(i * tile, tile)
        pltpu.make_async_copy(x_hbm.at[part], x_ref.at[part], sem.at[i]).wait()
        valid = len_ref[0, i // half_tiles] - (i % half_tiles) * tile

        @pl.when(valid < tile)
        def _():
            x = x_ref[part, :]
            position = lax.broadcasted_iota(jnp.int32, x.shape, 0)
            x_ref[part, :] = jnp.where(position < valid, x, jnp.zeros_like(x))

        total += jnp.sum(x_ref[part, :].astype(jnp.float32), axis=0, keepdims=True)
        product = dot_transposed(x_ref[part, 0:block], x_ref[part, :])
        if i:
            acc_ref[...] += product
        else:
            acc_ref[...] = product
    write_rows(
        (mine_ref, theirs_ref), [lambda owner, n: (acc_ref, 0, n * block)], me, members, rows, keys, pack
    )
    for n, key in enumerate(keys):
        sums_ref[0:1, block_columns(group, key, block)] = total[:, n * block:(n + 1) * block]
    count = (len_ref[0, 0] + len_ref[0, 1]).astype(jnp.float32)
    for ref in (mine_ref, theirs_ref):
        ref[pl.ds(block // 2, EXTRA), :] = jnp.full((EXTRA, width), count)
        for line, start in enumerate(range(0, width, pack)):
            size = min(pack, width - start)
            ref[pl.ds(block // 2 + line, 1), 0:size] = sums_ref[0:1, start:start + size]


def second_kernel(x_ref, acc_ref, *, block):
    acc_ref[...] = dot_transposed(x_ref[:, block:2 * block], x_ref[:, block:])


def third_kernel(me_ref, x_ref, first_ref, second_ref, after_ref, mine_ref, theirs_ref,
                 theirs_later_ref, mine_next_ref, theirs_next_ref, mine_last_ref, theirs_last_ref, acc_ref,
                 *, keys, members, rows, pack):
    block = members * rows

    def cut(n):
        return slice(n * block, (n + 1) * block)

    for n in (1, 2, 3):
        acc_ref[cut(n - 1), cut(0)] = first_ref[:, cut(n)].T
    acc_ref[cut(0), block:] = second_ref[...]
    for n in (2, 3):
        acc_ref[cut(n - 1), cut(1)] = second_ref[:, cut(n - 1)].T
    acc_ref[cut(1), 2 * block:] = dot_transposed(x_ref[:, cut(2)], x_ref[:, 2 * block:])
    acc_ref[cut(2), cut(3)] = dot_transposed(x_ref[:, cut(3)], x_ref[:, cut(3)])
    acc_ref[cut(2), cut(2)] = acc_ref[cut(1), cut(3)].T

    def step_one(owner, n):
        return acc_ref, owner * block, n * block

    def step_two(owner, n):
        return acc_ref, (1 - owner) * block, n * block

    def kept(owner, n):
        return acc_ref, 2 * block, n * block

    me = me_ref[0]
    write_rows((mine_ref, (theirs_ref, theirs_later_ref)), [step_one], me, members, rows, keys, pack)
    write_rows((mine_next_ref, theirs_next_ref), [step_two], me, members, rows, keys, pack)
    write_rows((mine_last_ref, theirs_last_ref), [kept], me, members, rows, keys, pack)


def total_of(refs, terms, height, size):
    parts = [refs[i][pl.ds(row, height), pl.ds(column, size)] for i, row, column in terms]
    return sum(parts[1:], parts[0])


def sum_kernel(*refs, plan, size):
    out = refs[-1]
    at = 0
    for height, terms in plan:
        out[pl.ds(at, height), :] = total_of(refs, terms, height, size)
        at += height


def finish_kernel(me_ref, *refs, chains, ranges, extra, rows):
    cov_ref, mean_ref, count_ref = refs[-3:]
    width = cov_ref.shape[1]
    pack = ranges[0][1]
    lines = -(-width // pack)
    block = total_of(refs, extra, EXTRA, pack)
    total = jnp.concatenate([block[i:i + 1] for i in range(lines)], axis=1)[:, :width]
    count = block[lines:lines + 1, 0:1]
    lane = lax.broadcasted_iota(jnp.int32, (rows, width), 1)
    row = lax.broadcasted_iota(jnp.int32, (rows, width), 0)
    own = jnp.sum(
        jnp.where(lane == row + me_ref[0] * rows, total, 0.0), axis=1, keepdims=True
    )
    mean = total / count
    mean_ref[...] = mean
    count_ref[...] = count
    for (start, size), terms in zip(ranges, chains):
        second = total_of(refs, terms, rows, size) - own * mean[:, start:start + size]
        cov_ref[:, start:start + size] = second / (count - 1.0)


def column_ranges(width, parts):
    tiles, ranges, start = width // LANES, [], 0
    for i in range(parts):
        size = (tiles + parts - 1 - i) // parts * LANES
        ranges.append((start, size))
        start += size
    return ranges


def limit(mebibytes):
    return pltpu.CompilerParams(vmem_limit_bytes=mebibytes << 20)


def solution(mesh):
    axes = ("grp", "mem")
    groups, members = mesh.shape["grp"], mesh.shape["mem"]
    devices = groups * members
    keys = (3, 1, 2, 0)
    assert groups == len(keys)
    near, far = member_masks(members)
    steps = [(members, 2 * members), (2 * members, members), *zip(near, far)]

    def swap(value, masks):
        pairs = [(i, i ^ masks[i % 2]) for i in range(devices)]
        return lax.ppermute(value, axes, pairs)

    def body(features, lengths):
        depth, width = features.shape
        rows = width // devices
        block = members * rows
        half = block // 2
        ranges = column_ranges(width, CHAINS)
        pack = ranges[0][1]
        me = (lax.axis_index("grp") * members + lax.axis_index("mem")).reshape(1)

        def f32(height, size=width):
            return jax.ShapeDtypeStruct((height, size), jnp.float32)

        def cost(blocks):
            return pl.CostEstimate(
                flops=2 * depth * block * block * blocks,
                bytes_accessed=depth * width * 2,
                transcendentals=0,
            )

        tile = depth // 4
        sizes = dict(keys=keys, members=members, rows=rows, pack=pack)
        mine, theirs, x, acc = pl.pallas_call(
            functools.partial(first_kernel, tile=tile, **sizes),
            out_shape=[f32(half + EXTRA)] * 2
            + [jax.ShapeDtypeStruct(features.shape, features.dtype), f32(block)],
            in_specs=[SMEM, HBM, HBM],
            out_specs=[VMEM] * 4,
            scratch_shapes=[
                pltpu.SMEM(lengths.shape, jnp.int32),
                pltpu.VMEM((EXTRA, width), jnp.float32),
                pltpu.SemaphoreType.DMA((depth // tile + 1,)),
            ],
            compiler_params=limit(40),
            cost_estimate=cost(4),
        )(me, lengths, features)
        arrays, narrow = [], []
        acc_next = pl.pallas_call(
            functools.partial(second_kernel, block=block),
            out_shape=jax.ShapeDtypeStruct((block, width - block), jnp.float32),
            in_specs=[VMEM],
            out_specs=VMEM,
            compiler_params=limit(32),
            cost_estimate=cost(3),
        )(x)

        def localise(used, terms, start):
            return [(used.index(i), row, 0 if narrow[i] else start) for i, row in terms]

        def total(plan, start, size, after=()):
            used = sorted({i for _, terms in plan for i, _ in terms}.union(after))
            plan = [(height, localise(used, terms, start)) for height, terms in plan]
            return pl.pallas_call(
                functools.partial(sum_kernel, plan=plan, size=size),
                out_shape=f32(sum(height for height, _ in plan), size),
                in_specs=[VMEM] * len(used),
                out_specs=VMEM,
                compiler_params=limit(12),
                cost_estimate=pl.CostEstimate(flops=1, bytes_accessed=1, transcendentals=0),
            )(*[arrays[i] for i in used])

        def put(array, wide=True):
            arrays.append(array)
            narrow.append(not wide)
            return len(arrays) - 1

        one, one_in = put(mine), put(swap(theirs, (1, 1)))
        extra = [(one, half), (one_in, half)]
        message = total([(half, [(one, 0), (one_in, 0)]), (EXTRA, extra)], 0, width)
        one_next = put(swap(message, steps[0]))
        mine, theirs, theirs_later, mine_next, theirs_next, mine_last, theirs_last = pl.pallas_call(
            functools.partial(third_kernel, **sizes),
            out_shape=[f32(half)] + [f32(half // 2)] * 2 + [f32(half)] * 4,
            in_specs=[SMEM] + [VMEM] * 4,
            out_specs=[VMEM] * 7,
            scratch_shapes=[pltpu.VMEM((3 * block, width), jnp.float32)],
            compiler_params=limit(32),
            cost_estimate=cost(3),
        )(me, x, acc, acc_next, message)
        two, two_in = put(mine), [put(swap(part, (1, 1))) for part in (theirs, theirs_later)]
        after, after_in = put(mine_next), put(swap(theirs_next, (1, 1)))
        last, last_in = put(mine_last), put(swap(theirs_last, (1, 1)))
        extra.append((one_next, half))
        both = [(half // 2, [(two, i * half // 2), (other, 0)]) for i, other in enumerate(two_in)]
        two_sent = [put(total(both, *columns), False) for columns in ranges]
        two_next = [put(swap(arrays[i], steps[0]), False) for i in two_sent]
        chains = []
        for (start, size), two_out in zip(ranges, two_next):
            carried = [] if start else [(EXTRA, extra)]
            message = total(
                [(half, [(after, 0), (after_in, 0), (one_next, 0)])] + carried, start, size, two_next[:1] if start else two_sent
            )
            added = put(swap(message, steps[1]), False)
            chains.append([(last, 0), (last_in, 0), (two_out, 0), (added, 0)])
            if not start:
                extra = extra + [(added, half)]
        height = half
        for masks in steps[2:]:
            height //= 2
            for c, (start, size) in enumerate(ranges):
                carried = [] if start else [(EXTRA, extra)]
                message = total([(height, chains[c])] + carried, start, size)
                added = put(swap(message, masks[::-1] if c else masks), False)
                chains[c] = [(i, row + height) for i, row in chains[c]] + [(added, 0)]
                if not start:
                    extra = extra + [(added, height)]

        used = sorted({i for terms in chains + [extra] for i, _ in terms})
        covariance, mean, count = pl.pallas_call(
            functools.partial(
                finish_kernel,
                chains=[localise(used, terms, start) for terms, (start, _) in zip(chains, ranges)],
                ranges=ranges,
                extra=localise(used, extra, 0),
                rows=rows,
            ),
            out_shape=[f32(rows), f32(1), jax.ShapeDtypeStruct((1, 1), jnp.float32)],
            in_specs=[SMEM] + [VMEM] * len(used),
            out_specs=[VMEM] * 3,
            compiler_params=limit(12),
            cost_estimate=pl.CostEstimate(flops=1, bytes_accessed=1, transcendentals=0),
        )(me, *[arrays[i] for i in used])
        return count.reshape(1), mean.reshape(width), covariance

    return jax.shard_map(
        body,
        mesh=mesh,
        in_specs=(P(axes, None), P(axes, None)),
        out_specs=(P(), P(), P(axes, None)),
        check_vma=False,
    )
```

```python
import functools

import jax
import jax.numpy as jnp
from jax import lax
from jax.experimental import pallas as pl
from jax.experimental.pallas import tpu as pltpu
from jax.sharding import PartitionSpec as P

LANES = 128
EXTRA = 8
CHAINS = 2
SMEM = pl.BlockSpec(memory_space=pltpu.SMEM)
VMEM = pl.BlockSpec(memory_space=pltpu.VMEM)
HBM = pl.BlockSpec(memory_space=pltpu.HBM)


def member_masks(members):
    return [1 << bit for bit in range(1, members.bit_length() - 1)]


def member_order(masks):
    order = []
    for place in range(1 << len(masks)):
        member = 0
        for i, mask in enumerate(masks):
            if not place >> (len(masks) - 1 - i) & 1:
                member ^= mask
        order.append(member)
    return order


def dot_transposed(a, b):
    return lax.dot_general(a, b, (((0,), (0,)), ((), ())), preferred_element_type=jnp.float32)


def block_columns(group, key, block):
    return pl.ds(pl.multiple_of((group ^ key) * block, block), block)


def write_rows(outs, chunks, me, members, rows, keys):
    group, member = me // members, me % members
    core = me % 2
    block = members * rows
    order = member_order(member_masks(members))
    for out, other in zip(outs, (0, 1)):
        owner = core ^ other
        for c, chunk in enumerate(chunks):
            for i, relative in enumerate(order):
                start = (member ^ other ^ relative) * rows
                place = (c * len(order) + i) * rows
                target = out
                if isinstance(out, tuple):
                    target = out[place // out[0].shape[0]]
                    place %= out[0].shape[0]
                at = pl.ds(place, rows)
                for n, key in enumerate(keys):
                    ref, row, column = chunk(owner, n)
                    source = pl.ds(pl.multiple_of(row + start, rows), rows)
                    target[at, block_columns(group, key, block)] = ref[source, pl.ds(column, block)]


def first_kernel(me_ref, len_hbm, x_hbm, mine_ref, theirs_ref, x_ref, acc_ref,
                 len_ref, sums_ref, sem, *, tile, keys, members, rows, pack):
    depth, width = x_hbm.shape
    block = members * rows
    tiles = depth // tile
    half_tiles = tiles // 2
    me = me_ref[0]
    group = me // members

    lengths = pltpu.make_async_copy(len_hbm, len_ref, sem.at[tiles])
    lengths.start()
    for i in range(tiles):
        part = pl.ds(i * tile, tile)
        for n, key in enumerate(keys):
            pltpu.make_async_copy(
                x_hbm.at[part, block_columns(group, key, block)],
                x_ref.at[part, pl.ds(n * block, block)],
                sem.at[i],
            ).start()
    lengths.wait()
    total = jnp.zeros((1, width), jnp.float32)
    for i in range(tiles):
        part = pl.ds(i * tile, tile)
        pltpu.make_async_copy(x_hbm.at[part], x_ref.at[part], sem.at[i]).wait()
        valid = len_ref[0, i // half_tiles] - (i % half_tiles) * tile

        @pl.when(valid < tile)
        def _():
            x = x_ref[part, :]
            position = lax.broadcasted_iota(jnp.int32, x.shape, 0)
            x_ref[part, :] = jnp.where(position < valid, x, jnp.zeros_like(x))

        total += jnp.sum(x_ref[part, :].astype(jnp.float32), axis=0, keepdims=True)
        product = dot_transposed(x_ref[part, 0:block], x_ref[part, :])
        if i:
            acc_ref[...] += product
        else:
            acc_ref[...] = product
    write_rows(
        (mine_ref, theirs_ref), [lambda owner, n: (acc_ref, 0, n * block)], me, members, rows, keys
    )
    for n, key in enumerate(keys):
        sums_ref[0:1, block_columns(group, key, block)] = total[:, n * block:(n + 1) * block]
    count = (len_ref[0, 0] + len_ref[0, 1]).astype(jnp.float32)
    for ref in (mine_ref, theirs_ref):
        ref[pl.ds(block // 2, EXTRA), :] = jnp.full((EXTRA, width), count)
        for line, start in enumerate(range(0, width, pack)):
            size = min(pack, width - start)
            ref[pl.ds(block // 2 + line, 1), 0:size] = sums_ref[0:1, start:start + size]


def second_kernel(x_ref, acc_ref, *, block):
    acc_ref[...] = dot_transposed(x_ref[:, block:2 * block], x_ref[:, block:])


def third_kernel(me_ref, x_ref, first_ref, second_ref, after_ref, mine_ref, theirs_ref,
                 theirs_later_ref, mine_next_ref, theirs_next_ref, mine_last_ref, theirs_last_ref, acc_ref,
                 *, keys, members, rows):
    block = members * rows

    def cut(n):
        return slice(n * block, (n + 1) * block)

    for n in (1, 2, 3):
        acc_ref[cut(n - 1), cut(0)] = first_ref[:, cut(n)].T
    acc_ref[cut(0), block:] = second_ref[...]
    for n in (2, 3):
        acc_ref[cut(n - 1), cut(1)] = second_ref[:, cut(n - 1)].T
    acc_ref[cut(1), 2 * block:] = dot_transposed(x_ref[:, cut(2)], x_ref[:, 2 * block:])
    acc_ref[cut(2), cut(3)] = dot_transposed(x_ref[:, cut(3)], x_ref[:, cut(3)])
    acc_ref[cut(2), cut(2)] = acc_ref[cut(1), cut(3)].T

    def step_one(owner, n):
        return acc_ref, owner * block, n * block

    def step_two(owner, n):
        return acc_ref, (1 - owner) * block, n * block

    def kept(owner, n):
        return acc_ref, 2 * block, n * block

    me = me_ref[0]
    write_rows((mine_ref, (theirs_ref, theirs_later_ref)), [step_one], me, members, rows, keys)
    write_rows((mine_next_ref, theirs_next_ref), [step_two], me, members, rows, keys)
    write_rows((mine_last_ref, theirs_last_ref), [kept], me, members, rows, keys)


def total_of(refs, terms, height, size):
    parts = [refs[i][pl.ds(row, height), pl.ds(column, size)] for i, row, column in terms]
    return sum(parts[1:], parts[0])


def sum_kernel(*refs, plan, size):
    out = refs[-1]
    at = 0
    for height, terms in plan:
        out[pl.ds(at, height), :] = total_of(refs, terms, height, size)
        at += height


def finish_kernel(me_ref, *refs, chains, ranges, extra, rows):
    cov_ref, mean_ref, count_ref = refs[-3:]
    width = cov_ref.shape[1]
    pack = ranges[0][1]
    lines = -(-width // pack)
    block = total_of(refs, extra, EXTRA, pack)
    total = jnp.concatenate([block[i:i + 1] for i in range(lines)], axis=1)[:, :width]
    count = block[lines:lines + 1, 0:1]
    lane = lax.broadcasted_iota(jnp.int32, (rows, width), 1)
    row = lax.broadcasted_iota(jnp.int32, (rows, width), 0)
    own = jnp.sum(
        jnp.where(lane == row + me_ref[0] * rows, total, 0.0), axis=1, keepdims=True
    )
    mean = total / count
    mean_ref[...] = mean
    count_ref[...] = count
    for (start, size), terms in zip(ranges, chains):
        second = total_of(refs, terms, rows, size) - own * mean[:, start:start + size]
        cov_ref[:, start:start + size] = second / (count - 1.0)


def column_ranges(width, parts):
    tiles, ranges, start = width // LANES, [], 0
    for i in range(parts):
        size = (tiles + parts - 1 - i) // parts * LANES
        ranges.append((start, size))
        start += size
    return ranges


def limit(mebibytes):
    return pltpu.CompilerParams(vmem_limit_bytes=mebibytes << 20)


def solution(mesh):
    axes = ("grp", "mem")
    groups, members = mesh.shape["grp"], mesh.shape["mem"]
    devices = groups * members
    keys = (3, 2, 1, 0)
    assert groups == len(keys)
    steps = [(2 * members, members), (members, 2 * members)]
    steps += [(mask, mask) for mask in member_masks(members)]

    def swap(value, masks):
        pairs = [(i, i ^ masks[i % 2]) for i in range(devices)]
        return lax.ppermute(value, axes, pairs)

    def body(features, lengths):
        depth, width = features.shape
        rows = width // devices
        block = members * rows
        half = block // 2
        ranges = column_ranges(width, CHAINS)
        pack = ranges[0][1]
        me = (lax.axis_index("grp") * members + lax.axis_index("mem")).reshape(1)

        def f32(height, size=width):
            return jax.ShapeDtypeStruct((height, size), jnp.float32)

        def cost(blocks):
            return pl.CostEstimate(
                flops=2 * depth * block * block * blocks,
                bytes_accessed=depth * width * 2,
                transcendentals=0,
            )

        tile = depth // 4
        sizes = dict(keys=keys, members=members, rows=rows)
        mine, theirs, x, acc = pl.pallas_call(
            functools.partial(first_kernel, tile=tile, pack=pack, **sizes),
            out_shape=[f32(half + EXTRA)] * 2
            + [jax.ShapeDtypeStruct(features.shape, features.dtype), f32(block)],
            in_specs=[SMEM, HBM, HBM],
            out_specs=[VMEM] * 4,
            scratch_shapes=[
                pltpu.SMEM(lengths.shape, jnp.int32),
                pltpu.VMEM((EXTRA, width), jnp.float32),
                pltpu.SemaphoreType.DMA((depth // tile + 1,)),
            ],
            compiler_params=limit(40),
            cost_estimate=cost(4),
        )(me, lengths, features)
        arrays, narrow = [], []
        acc_next = pl.pallas_call(
            functools.partial(second_kernel, block=block),
            out_shape=jax.ShapeDtypeStruct((block, width - block), jnp.float32),
            in_specs=[VMEM],
            out_specs=VMEM,
            compiler_params=limit(32),
            cost_estimate=cost(3),
        )(x)

        def localise(used, terms, start):
            return [(used.index(i), row, 0 if narrow[i] else start) for i, row in terms]

        def total(plan, start, size, after=()):
            used = sorted({i for _, terms in plan for i, _ in terms}.union(after))
            plan = [(height, localise(used, terms, start)) for height, terms in plan]
            return pl.pallas_call(
                functools.partial(sum_kernel, plan=plan, size=size),
                out_shape=f32(sum(height for height, _ in plan), size),
                in_specs=[VMEM] * len(used),
                out_specs=VMEM,
                compiler_params=limit(12),
                cost_estimate=pl.CostEstimate(flops=1, bytes_accessed=1, transcendentals=0),
            )(*[arrays[i] for i in used])

        def put(array, wide=True):
            arrays.append(array)
            narrow.append(not wide)
            return len(arrays) - 1

        one, one_in = put(mine), put(swap(theirs, (1, 1)))
        extra = [(one, half), (one_in, half)]
        message = total([(half, [(one, 0), (one_in, 0)]), (EXTRA, extra)], 0, width)
        one_next = put(swap(message, steps[0]))
        mine, theirs, theirs_later, mine_next, theirs_next, mine_last, theirs_last = pl.pallas_call(
            functools.partial(third_kernel, **sizes),
            out_shape=[f32(half)] + [f32(half // 2)] * 2 + [f32(half)] * 4,
            in_specs=[SMEM] + [VMEM] * 4,
            out_specs=[VMEM] * 7,
            scratch_shapes=[pltpu.VMEM((3 * block, width), jnp.float32)],
            compiler_params=limit(32),
            cost_estimate=cost(3),
        )(me, x, acc, acc_next, message)
        two, two_in = put(mine), [put(swap(part, (1, 1))) for part in (theirs, theirs_later)]
        after, after_in = put(mine_next), put(swap(theirs_next, (1, 1)))
        last, last_in = put(mine_last), put(swap(theirs_last, (1, 1)))
        extra.append((one_next, half))
        both = [(half // 2, [(two, i * half // 2), (other, 0)]) for i, other in enumerate(two_in)]
        two_sent = [put(total(both, *columns), False) for columns in ranges]
        two_next = [put(swap(arrays[i], steps[0]), False) for i in two_sent]
        chains = []
        for (start, size), two_out in zip(ranges, two_next):
            carried = [] if start else [(EXTRA, extra)]
            message = total(
                [(half, [(after, 0), (after_in, 0), (one_next, 0)])] + carried, start, size, two_next[:1] if start else two_sent
            )
            added = put(swap(message, steps[1]), False)
            chains.append([(last, 0), (last_in, 0), (two_out, 0), (added, 0)])
            if not start:
                extra = extra + [(added, half)]
        height = half
        for masks in steps[2:]:
            height //= 2
            for c, (start, size) in enumerate(ranges):
                carried = [] if start else [(EXTRA, extra)]
                message = total([(height, chains[c])] + carried, start, size)
                added = put(swap(message, masks), False)
                chains[c] = [(i, row + height) for i, row in chains[c]] + [(added, 0)]
                if not start:
                    extra = extra + [(added, height)]

        used = sorted({i for terms in chains + [extra] for i, _ in terms})
        covariance, mean, count = pl.pallas_call(
            functools.partial(
                finish_kernel,
                chains=[localise(used, terms, start) for terms, (start, _) in zip(chains, ranges)],
                ranges=ranges,
                extra=localise(used, extra, 0),
                rows=rows,
            ),
            out_shape=[f32(rows), f32(1), jax.ShapeDtypeStruct((1, 1), jnp.float32)],
            in_specs=[SMEM] + [VMEM] * len(used),
            out_specs=[VMEM] * 3,
            compiler_params=limit(12),
            cost_estimate=pl.CostEstimate(flops=1, bytes_accessed=1, transcendentals=0),
        )(me, *[arrays[i] for i in used])
        return count.reshape(1), mean.reshape(width), covariance

    return jax.shard_map(
        body,
        mesh=mesh,
        in_specs=(P(axes, None), P(axes, None)),
        out_specs=(P(), P(), P(axes, None)),
        check_vma=False,
    )
```
